128 devices in a mesh: section: 4 (over x_hi, core), shard: 32 (over x_lo, z, y).
Axes of the slice: x: 4 (x_hi: 2, x_lo: 2; x = x_hi * 2 + x_lo), y: 4, z: 4, core: 2. Of those that a mesh axis runs over, the one named last changes fastest.
Arguments:
- hidden: bfloat16 [1024, 8192], P(('section', 'shard')), may hold values from -6 to 6
- norm_gain: float32 [4, 8192], P('section'), may hold values from 0.1 to 1.9
- gate_weight: bfloat16 [4, 8192, 16384], P('section', None, 'shard'), may hold values from -0.0625 to 0.0625
- up_weight: bfloat16 [4, 8192, 16384], P('section', None, 'shard'), may hold values from -0.0625 to 0.0625
- head_vector: bfloat16 [4, 16384], P('section', 'shard'), may hold values from -0.046875 to 0.046875
- pack_slot: int32 [4, 1024], replicated, may hold values from 0 to 1023, each once within a row
- owner_slot: int32 [1024], replicated, may hold values from 0 to 1023, each once
Outputs:
- section_scores: float32 [4, 1024], P('section', 'shard')
- joined: float32 [4, 1024], P(None, ('section', 'shard'))
The draws below stay inside these ranges and needn't reach their ends.
All inputs are finite; a program needn't handle non-finite values.
Results may differ from the reference program's by a relative error of at most 0.0032.
Values may be sent and summed in bfloat16 or wider, within the bound.
No kernel may reach another device: no remote copies, remote signals or barrier semaphores. Data moves between devices by JAX's collectives and lax.ppermute only.
A program may use at most 128 MiB of HBM per device.

```python
import jax
import jax.numpy as jnp
from jax import lax

D = 8192
FFW = 16384
ROWS = 1024


def block_scale(key, dims, shards, least, largest):
    level, own = 1.0, jax.random.fold_in(key, 6)
    for axis_at, blocks in shards:
        heights = jnp.exp(jax.random.uniform(jax.random.fold_in(own, axis_at), (blocks,), jnp.float32, least / len(shards), largest / len(shards)))
        level = level * jnp.repeat(heights, dims[axis_at] // blocks).reshape([-1 if axis == axis_at else 1 for axis in range(len(dims))])
    return level


def scatter_about(rng, shape, deviation, reach, pieces=(), dtype=jnp.bfloat16):
    factor_of = block_scale(rng, shape, pieces, -0.22, 0.18) if pieces else 1.0
    entries = jax.random.normal(rng, shape, jnp.float32) * deviation * factor_of
    return jnp.minimum(jnp.maximum(entries, -reach), reach).astype(dtype)


def setup_inputs(seed: int = 0) -> dict:
    streams_of = jax.random.split(jax.random.key(seed), 8)
    return {
        "hidden": scatter_about(streams_of[0], (ROWS, D), 1.0, 6.0, ((0, 128),)),
        "norm_gain": jnp.clip(1.0 + 0.18 * jax.random.normal(streams_of[1], (4, D), jnp.float32), 0.1, 1.9),
        "gate_weight": scatter_about(streams_of[2], (4, D, FFW), D ** -0.5, 0.0625, ((0, 4), (2, 32))),
        "up_weight": scatter_about(streams_of[3], (4, D, FFW), D ** -0.5, 0.0625, ((0, 4), (2, 32))),
        "head_vector": scatter_about(streams_of[4], (4, FFW), FFW ** -0.5, 0.046875, ((0, 4), (1, 32))),
        "pack_slot": jax.vmap(lambda own: jax.random.permutation(own, ROWS))(jax.random.split(streams_of[5], 4)).reshape((4, ROWS)).astype(jnp.int32),
        "owner_slot": jax.random.permutation(streams_of[6], ROWS).astype(jnp.int32),
    }


epsilon = 1e-06

def reference(hidden, norm_gain, gate_weight, up_weight, head_vector, pack_slot, owner_slot):
    widened = hidden.astype(jnp.float32)
    inv_rms = lax.rsqrt(lax.optimization_barrier(jnp.mean(widened * widened, axis=1, keepdims=True)) + epsilon)
    section_outputs = []
    joined = jnp.zeros((4, ROWS), jnp.float32)
    for section in range(4):
        normed = (widened * inv_rms * norm_gain[section]).astype(jnp.bfloat16)
        gate_out = jnp.dot(normed, gate_weight[section], preferred_element_type=jnp.float32)
        up_out = jnp.dot(normed, up_weight[section], preferred_element_type=jnp.float32)
        activated = jax.nn.silu(gate_out) * up_out
        scores = jnp.dot(activated, head_vector[section].astype(jnp.float32), precision=lax.Precision.HIGHEST)
        if section == 1 or section == 3:
            scores = jax.nn.log_sigmoid(scores)
        packed = jnp.zeros((ROWS,), jnp.float32).at[pack_slot[section]].set(scores)
        section_outputs.append(packed)
        joined = joined.at[section, owner_slot].set(scores)
    return (jnp.stack(section_outputs), joined)
```

```python
import functools

import jax
import jax.numpy as jnp
from jax import lax
from jax.experimental import pallas as pl
from jax.experimental.pallas import tpu as pltpu
from jax.sharding import Mesh, PartitionSpec as P

epsilon = 1e-06
ALL = ("xh", "core", "xl", "z", "y")
ORDER = (("y", "x", "z"), ("x", "z", "y"))
ROWS = 256
STEP = 1024


def flat_index(x, y, z, core):
    return (x // 2) * 64 + core * 32 + (x % 2) * 16 + z * 4 + y


def shift_pairs(phase, step):
    pairs = []
    for core in range(2):
        at = "xyz".index(ORDER[core][phase])
        for x in range(4):
            for y in range(4):
                for z in range(4):
                    to = [x, y, z]
                    to[at] = (to[at] + step) % 4
                    pairs.append((flat_index(x, y, z, core), flat_index(*to, core)))
    return pairs


def shift(block, phase, step):
    return lax.ppermute(block, ALL, shift_pairs(phase, step))


def sibling(block):
    return lax.ppermute(block, "core", [(0, 1), (1, 0)])


def stage_kernel(pieces, features, *refs):
    rows = refs[:pieces]
    gate_ref, up_ref, head_ref, column_ref, row_ref, before_ref, out_ref, gate_sum, up_sum, square_sum = refs[pieces:]
    step = pl.program_id(0)

    @pl.when(step == 0)
    def _():
        gate_sum[...] = jnp.zeros_like(gate_sum)
        up_sum[...] = jnp.zeros_like(up_sum)
        square_sum[...] = jnp.zeros_like(square_sum)

    block = jnp.concatenate([ref[...] for ref in rows], axis=0)
    gate_sum[...] += jnp.dot(block, gate_ref[...], preferred_element_type=jnp.float32)
    up_sum[...] += jnp.dot(block, up_ref[...], preferred_element_type=jnp.float32)
    total = square_sum[...]
    for at in range(0, STEP, 128):
        part = block[:, at : at + 128].astype(jnp.float32)
        total = total + part * part
    square_sum[...] = total

    @pl.when(step == pl.num_programs(0) - 1)
    def _():
        mean = jnp.sum(square_sum[...], axis=1, keepdims=True) / features
        inv_rms = lax.rsqrt(mean + epsilon)
        gate = gate_sum[...] * inv_rms
        up = up_sum[...] * inv_rms
        activated = gate / (1.0 + jnp.exp(-gate)) * up
        score = jnp.sum(activated * head_ref[...], axis=1, keepdims=True)
        lane = lax.broadcasted_iota(jnp.int32, (ROWS, 128), 1)
        line = lax.broadcasted_iota(jnp.int32, (128, ROWS), 0)
        owner_part = jnp.where(column_ref[:, 0:1] == lane, score, 0.0)
        pack_part = jnp.where(column_ref[:, 1:2] == lane, score, 0.0)
        owner_line = jnp.where(row_ref[0:1, :] == line, 1.0, 0.0)
        pack_line = jnp.where(row_ref[1:2, :] == line, 1.0, 0.0)
        out_ref[...] = (
            before_ref[...]
            + jnp.dot(owner_line, owner_part, precision=lax.Precision.HIGHEST, preferred_element_type=jnp.float32)
            + jnp.dot(pack_line, pack_part, precision=lax.Precision.HIGHEST, preferred_element_type=jnp.float32)
        )


def stage(rows, gate, up, head, column, row, before):
    features, width = gate.shape
    return pl.pallas_call(
        functools.partial(stage_kernel, len(rows), features),
        grid=(features // STEP,),
        out_shape=jax.ShapeDtypeStruct((128, 128), jnp.float32),
        in_specs=[pl.BlockSpec((piece.shape[0], STEP), lambda k: (0, k)) for piece in rows]
        + [pl.BlockSpec((STEP, width), lambda k: (k, 0))] * 2
        + [
            pl.BlockSpec((1, width), lambda k: (0, 0)),
            pl.BlockSpec(column.shape, lambda k: (0, 0)),
            pl.BlockSpec(row.shape, lambda k: (0, 0)),
            pl.BlockSpec((128, 128), lambda k: (0, 0)),
        ],
        out_specs=pl.BlockSpec((128, 128), lambda k: (0, 0)),
        scratch_shapes=[
            pltpu.VMEM((ROWS, width), jnp.float32),
            pltpu.VMEM((ROWS, width), jnp.float32),
            pltpu.VMEM((ROWS, 128), jnp.float32),
        ],
        compiler_params=pltpu.CompilerParams(vmem_limit_bytes=32 * 1024 * 1024),
        cost_estimate=pl.CostEstimate(flops=4 * ROWS * features * width, bytes_accessed=4 * features * width, transcendentals=ROWS * width),
    )(*rows, gate, up, head, column, row, before)


def tokens_of(core, third):
    place = {"x": lax.axis_index("xh") * 2 + lax.axis_index("xl"), "y": lax.axis_index("y"), "z": lax.axis_index("z")}
    at = jnp.arange(128, dtype=jnp.int32)
    back = (at // 8 % 4, at // 32, third)
    token = []
    for half in range(2):
        source = {axis: (place[axis] - back[phase]) % 4 for phase, axis in enumerate(ORDER[half])}
        token.append(flat_index(source["x"], source["y"], source["z"], half) * 8 + at % 8)
    return jnp.where(core == 0, token[0], token[1])


def body(hidden, norm_gain, gate_weight, up_weight, head_vector, pack_slot, owner_slot):
    core = lax.axis_index("core")
    section = lax.axis_index("xh") * 2 + core
    gain = norm_gain[0][:, None]
    gate = (gate_weight[0].astype(jnp.float32) * gain).astype(jnp.bfloat16)
    up = (up_weight[0].astype(jnp.float32) * gain).astype(jnp.bfloat16)
    head = head_vector.astype(jnp.float32)
    own_pack = lax.dynamic_index_in_dim(pack_slot, section, 0, keepdims=False)

    line = jnp.concatenate([hidden] + [shift(hidden, 0, step) for step in (1, 2, 3)], axis=0)
    plane = jnp.concatenate([line] + [shift(line, 1, step) for step in (1, 2, 3)], axis=0)
    behind = shift(plane, 2, 1)
    ahead = shift(plane, 2, 3)
    far_low = shift(behind[:64], 2, 1)
    far_high = shift(ahead[64:], 2, 3)
    groups = ((0, (plane,)), (1, (behind,)), (3, (ahead,)), (2, (far_low, far_high)))

    sent = jnp.zeros((128, 128), jnp.float32)
    for third, pieces in groups:
        rows = list(pieces) + [sibling(piece) for piece in pieces]
        token = jnp.concatenate([tokens_of(core, third), tokens_of(1 - core, third)])
        owner, pack = owner_slot[token], own_pack[token]
        column = jnp.stack([owner % 8, pack % 32 + 8], axis=1)
        row = jnp.stack([owner // 8, pack // 32 + 32 * section], axis=0)
        sent = stage(rows, gate, up, head, column, row, sent)

    arrived = lax.all_to_all(sent[:, None, :], ALL, split_axis=0, concat_axis=0, tiled=True)
    sums = arrived.reshape(4, 32, 128).sum(axis=1)
    flipped = lax.broadcasted_iota(jnp.int32, (4, 8), 0) % 2 == 1
    joined = sums[:, :8]
    joined = jnp.where(flipped, jax.nn.log_sigmoid(joined), joined)
    scores = sums[:, 8:40].sum(axis=0, keepdims=True)
    scores = jnp.where(section % 2 == 1, jax.nn.log_sigmoid(scores), scores)
    return scores, joined


def solution(mesh):
    parts = Mesh(mesh.devices.reshape(2, 2, 2, 4, 4), ALL)
    section, shard = ("xh", "core"), ("xl", "z", "y")
    in_specs = (
        P(section + shard, None),
        P(section, None),
        P(section, None, shard),
        P(section, None, shard),
        P(section, shard),
        P(),
        P(),
    )
    out_specs = (P(section, shard), P(None, section + shard))
    return jax.shard_map(body, mesh=parts, in_specs=in_specs, out_specs=out_specs, check_vma=False)
```

```python
import functools

import jax
import jax.numpy as jnp
from jax import lax
from jax.experimental import pallas as pl
from jax.experimental.pallas import tpu as pltpu
from jax.sharding import Mesh, PartitionSpec as P

epsilon = 1e-06
ALL = ("xh", "core", "xl", "z", "y")
ORDER = (("y", "x", "z"), ("x", "z", "y"))
ROWS = 256
FOLD = 1024
SCOPED = 12 * 1024 * 1024


def flat_index(x, y, z, core):
    return (x // 2) * 64 + core * 32 + (x % 2) * 16 + z * 4 + y


def shift_pairs(phase, step):
    pairs = []
    for core in range(2):
        at = "xyz".index(ORDER[core][phase])
        for x in range(4):
            for y in range(4):
                for z in range(4):
                    to = [x, y, z]
                    to[at] = (to[at] + step) % 4
                    pairs.append((flat_index(x, y, z, core), flat_index(*to, core)))
    return pairs


def shift(block, phase, step):
    return lax.ppermute(block, ALL, shift_pairs(phase, step))


def sibling(block):
    return lax.ppermute(block, "core", [(0, 1), (1, 0)])


def fold_kernel(gate_ref, up_ref, gain_ref, code_ref, out_ref, spread_ref, sems):
    features, width = gate_ref.shape
    for block in range(features // FOLD):
        at = pl.ds(block * FOLD, FOLD)
        for half, ref in enumerate((gate_ref, up_ref)):
            pltpu.make_async_copy(ref.at[at, :], out_ref.at[half, at, :], sems.at[half, block]).start()

    for row in range(code_ref.shape[0]):
        code = jnp.broadcast_to(code_ref[row : row + 1, :].astype(jnp.float32), (128, 128))
        spread_ref[row * 128 : row * 128 + 128, :] = jnp.transpose(code, (1, 0)).astype(jnp.int32)

    @pl.loop(0, features // FOLD)
    def _(block):
        for half, ref in enumerate((gate_ref, up_ref)):
            at = pl.ds(pl.multiple_of(block * FOLD, FOLD), FOLD)
            pltpu.make_async_copy(ref.at[at, :], out_ref.at[half, at, :], sems.at[half, block]).wait()
        for part in range(FOLD // 128):
            at = pl.multiple_of(block * FOLD + part * 128, 128)
            gain = jnp.transpose(jnp.broadcast_to(gain_ref[:, pl.ds(at, 128)], (128, 128)), (1, 0))
            gain = jnp.concatenate([gain] * (width // 128), axis=1)
            for half in range(2):
                value = out_ref[half, pl.ds(at, 128), :].astype(jnp.float32)
                out_ref[half, pl.ds(at, 128), :] = (value * gain).astype(jnp.bfloat16)


def fold(gate, up, gain, code):
    features, width = gate.shape
    gate, up = (pltpu.with_memory_space_constraint(half, pltpu.HBM) for half in (gate, up))
    return pl.pallas_call(
        fold_kernel,
        out_shape=(pltpu.VMEM((2, features, width), jnp.bfloat16), pltpu.VMEM((code.size, 128), jnp.int32)),
        in_specs=[pl.BlockSpec(memory_space=pltpu.HBM)] * 2 + [pl.BlockSpec(memory_space=pltpu.VMEM)] * 2,
        out_specs=(pl.BlockSpec(memory_space=pltpu.VMEM),) * 2,
        scratch_shapes=[pltpu.SemaphoreType.DMA((2, features // FOLD))],
        compiler_params=pltpu.CompilerParams(vmem_limit_bytes=SCOPED),
        cost_estimate=pl.CostEstimate(flops=2 * features * width, bytes_accessed=4 * features * width, transcendentals=0),
    )(gate, up, gain, code)


def stage_kernel(number, pieces, *refs):
    rows = refs[:pieces]
    weight_ref, head_ref, code_ref, unit_ref, before_ref, out_ref, block_ref = refs[pieces:]
    features = block_ref.shape[1]
    first, squares = 0, []
    for ref in rows:
        count = ref.shape[0]
        for at in range(0, count, 64):
            total = jnp.zeros((64, 128), jnp.float32)
            for lane in range(0, features, 128):
                part = ref[at : at + 64, lane : lane + 128]
                block_ref[first + at : first + at + 64, lane : lane + 128] = part
                part = part.astype(jnp.float32)
                total = total + part * part
            squares.append(jnp.sum(total, axis=1, keepdims=True))
        first += count
    inv_rms = lax.rsqrt(jnp.concatenate(squares, axis=0) / features + epsilon)

    gate = jnp.dot(block_ref[...], weight_ref[0], preferred_element_type=jnp.float32) * inv_rms
    up = jnp.dot(block_ref[...], weight_ref[1], preferred_element_type=jnp.float32) * inv_rms
    activated = gate / (1.0 + jnp.exp(-gate)) * up
    score = jnp.sum(activated * head_ref[...], axis=1, keepdims=True)

    units = ROWS // 8
    code = jnp.concatenate(
        [code_ref[pl.ds(pl.multiple_of(unit_ref[number * units + at] * 8, 8), 8), :] for at in range(units)], axis=0
    )
    owner, pack = code // 1024, code % 1024
    section = unit_ref[128]
    lane = lax.broadcasted_iota(jnp.int32, (ROWS, 128), 1)
    line = jnp.concatenate([owner // 8 == lane, pack // 32 + 32 * section == lane], axis=0)
    line = jnp.where(line, 1.0, 0.0).astype(jnp.bfloat16)
    slot = jnp.concatenate(
        [jnp.where(owner % 8 == lane, score, 0.0), jnp.where(pack % 32 + 8 == lane, score, 0.0)], axis=0
    )
    terms = []
    for _ in range(3):
        terms.append(slot.astype(jnp.bfloat16))
        slot = slot - terms[-1].astype(jnp.float32)
    placed = lax.dot_general(
        line, jnp.concatenate(terms, axis=1), (((0,), (0,)), ((), ())), preferred_element_type=jnp.float32
    )
    out_ref[...] = before_ref[...] + placed[:, 0:128] + placed[:, 128:256] + placed[:, 256:384]


def stage(number, rows, weight, head, code, unit, before):
    _, features, width = weight.shape
    vmem = pl.BlockSpec(memory_space=pltpu.VMEM)
    rows = [pltpu.with_memory_space_constraint(piece, pltpu.VMEM) for piece in rows]
    weight = pltpu.with_memory_space_constraint(weight, pltpu.VMEM)
    code = pltpu.with_memory_space_constraint(code, pltpu.VMEM)
    return pl.pallas_call(
        functools.partial(stage_kernel, number, len(rows)),
        out_shape=jax.ShapeDtypeStruct((128, 128), jnp.float32),
        in_specs=[vmem] * (len(rows) + 3) + [pl.BlockSpec(memory_space=pltpu.SMEM), vmem],
        out_specs=vmem,
        scratch_shapes=[pltpu.VMEM((ROWS, features), jnp.bfloat16)],
        compiler_params=pltpu.CompilerParams(vmem_limit_bytes=SCOPED),
        cost_estimate=pl.CostEstimate(flops=4 * ROWS * features * width, bytes_accessed=4 * features * width, transcendentals=ROWS * width),
    )(*rows, weight, head, code, unit, before)


def unit_table(core, section):
    place = {"x": lax.axis_index("xh") * 2 + lax.axis_index("xl"), "y": lax.axis_index("y"), "z": lax.axis_index("z")}
    at = jnp.arange(128, dtype=jnp.int32)
    number = at // 32
    third = jnp.where(number < 2, number, 5 - number)
    back = (at % 4, at // 4 % 4, third)
    half = jnp.where(at // 16 % 2 == 0, core, 1 - core)
    device = []
    for kind in range(2):
        source = {axis: (place[axis] - back[phase]) % 4 for phase, axis in enumerate(ORDER[kind])}
        device.append(flat_index(source["x"], source["y"], source["z"], kind))
    table = jnp.where(half == 0, device[0], device[1])
    return jnp.concatenate([table, jnp.broadcast_to(section, (128,)).astype(jnp.int32)])


def finish_kernel(arrived_ref, unit_ref, scores_ref, joined_ref):
    def log_sigmoid(value):
        return jnp.minimum(value, 0.0) - jnp.log1p(jnp.exp(-jnp.abs(value)))

    sums = jnp.concatenate(
        [jnp.sum(arrived_ref[at : at + 32, :], axis=0, keepdims=True) for at in range(0, 128, 32)], axis=0
    )
    flipped = lax.broadcasted_iota(jnp.int32, sums.shape, 0) % 2 == 1
    joined_ref[...] = jnp.where(flipped, log_sigmoid(sums), sums)[:, 0:8]
    scores = jnp.sum(sums, axis=0, keepdims=True)
    scores_ref[...] = jnp.where(unit_ref[128] % 2 == 1, log_sigmoid(scores), scores)[:, 8:40]


def finish(arrived, unit):
    vmem = pl.BlockSpec(memory_space=pltpu.VMEM)
    return pl.pallas_call(
        finish_kernel,
        out_shape=(jax.ShapeDtypeStruct((1, 32), jnp.float32), jax.ShapeDtypeStruct((4, 8), jnp.float32)),
        in_specs=[vmem, pl.BlockSpec(memory_space=pltpu.SMEM)],
        out_specs=(vmem, vmem),
        compiler_params=pltpu.CompilerParams(vmem_limit_bytes=SCOPED),
    )(arrived, unit)


def exchange(sent):
    return lax.all_to_all(sent[:, None, :], ALL, split_axis=0, concat_axis=0, tiled=True).reshape(128, 128)


def body(hidden, norm_gain, gate_weight, up_weight, head_vector, pack_slot, owner_slot):
    core = lax.axis_index("core")
    section = lax.axis_index("xh") * 2 + core
    head = head_vector.astype(jnp.float32)
    own_pack = lax.dynamic_index_in_dim(pack_slot, section, 0, keepdims=False)
    code = (owner_slot * 1024 + own_pack).reshape(8, 128)
    unit = unit_table(core, section)
    sent = jnp.zeros((128, 128), jnp.float32)

    line = jnp.concatenate([hidden] + [shift(hidden, 0, step) for step in (1, 2, 3)], axis=0)
    line, gate, up, code, unit, head, sent = lax.optimization_barrier(
        (line, gate_weight[0], up_weight[0], code, unit, head, sent)
    )
    plane = jnp.concatenate([line] + [shift(line, 1, step) for step in (1, 2, 3)], axis=0)
    weight, code = fold(gate, up, norm_gain, code)
    plane, weight, code = lax.optimization_barrier((plane, weight, code))
    other = sibling(plane)
    behind = shift(plane, 2, 1)
    ahead = shift(plane, 2, 3)
    sent, _ = lax.optimization_barrier((sent, plane))
    sent = exchange(sent)
    sent = stage(0, (plane, other), weight, head, code, unit, sent)
    behind, ahead, sent = lax.optimization_barrier((behind, ahead, sent))
    other_behind, other_ahead = sibling(behind), sibling(ahead)
    far_low = shift(behind[:64], 2, 1)
    far_high = shift(ahead[64:], 2, 3)
    sent = stage(1, (behind, other_behind), weight, head, code, unit, sent)
    sent = stage(2, (ahead, other_ahead), weight, head, code, unit, sent)
    far_low, far_high, sent = lax.optimization_barrier((far_low, far_high, sent))
    far = (far_low, far_high, sibling(far_low), sibling(far_high))
    sent = stage(3, far, weight, head, code, unit, sent)

    return finish(exchange(sent), unit)


def solution(mesh):
    parts = Mesh(mesh.devices.reshape(2, 2, 2, 4, 4), ALL)
    section, shard = ("xh", "core"), ("xl", "z", "y")
    in_specs = (
        P(section + shard, None),
        P(section, None),
        P(section, None, shard),
        P(section, None, shard),
        P(section, shard),
        P(),
        P(),
    )
    out_specs = (P(section, shard), P(None, section + shard))
    return jax.shard_map(body, mesh=parts, in_specs=in_specs, out_specs=out_specs, check_vma=False)
```

```python
import functools

import jax
import jax.numpy as jnp
from jax import lax
from jax.experimental import pallas as pl
from jax.experimental.pallas import tpu as pltpu
from jax.sharding import Mesh, PartitionSpec as P

epsilon = 1e-06
ALL = ("xh", "core", "xl", "z", "y")
ORDER = (("y", "x", "z"), ("x", "z", "y"))
FOLD = 1024
SCOPED = 12 * 1024 * 1024


def flat_index(x, y, z, core):
    return (x // 2) * 64 + core * 32 + (x % 2) * 16 + z * 4 + y


def shift_pairs(phase, step):
    pairs = []
    for core in range(2):
        at = "xyz".index(ORDER[core][phase])
        for x in range(4):
            for y in range(4):
                for z in range(4):
                    to = [x, y, z]
                    to[at] = (to[at] + step) % 4
                    pairs.append((flat_index(x, y, z, core), flat_index(*to, core)))
    return pairs


def shift(block, phase, step):
    return lax.ppermute(block, ALL, shift_pairs(phase, step))


def sibling(block):
    return lax.ppermute(block, "core", [(0, 1), (1, 0)])


def fold_kernel(gate_ref, up_ref, gain_ref, code_ref, out_ref, spread_ref, sems):
    features, width = gate_ref.shape
    for block in range(features // FOLD):
        at = pl.ds(block * FOLD, FOLD)
        for half, ref in enumerate((gate_ref, up_ref)):
            pltpu.make_async_copy(ref.at[at, :], out_ref.at[half, at, :], sems.at[half, block]).start()

    for row in range(code_ref.shape[0]):
        code = jnp.broadcast_to(code_ref[row : row + 1, :].astype(jnp.float32), (128, 128))
        spread_ref[row * 128 : row * 128 + 128, :] = jnp.transpose(code, (1, 0)).astype(jnp.int32)

    @pl.loop(0, features // FOLD)
    def _(block):
        for half, ref in enumerate((gate_ref, up_ref)):
            at = pl.ds(pl.multiple_of(block * FOLD, FOLD), FOLD)
            pltpu.make_async_copy(ref.at[at, :], out_ref.at[half, at, :], sems.at[half, block]).wait()
        for part in range(FOLD // 128):
            at = pl.multiple_of(block * FOLD + part * 128, 128)
            gain = jnp.transpose(jnp.broadcast_to(gain_ref[:, pl.ds(at, 128)], (128, 128)), (1, 0))
            gain = jnp.concatenate([gain] * (width // 128), axis=1)
            for half in range(2):
                value = out_ref[half, pl.ds(at, 128), :].astype(jnp.float32)
                out_ref[half, pl.ds(at, 128), :] = (value * gain).astype(jnp.bfloat16)


def fold(gate, up, gain, code):
    features, width = gate.shape
    gate, up = (pltpu.with_memory_space_constraint(half, pltpu.HBM) for half in (gate, up))
    return pl.pallas_call(
        fold_kernel,
        out_shape=(pltpu.VMEM((2, features, width), jnp.bfloat16), pltpu.VMEM((code.size, 128), jnp.int32)),
        in_specs=[pl.BlockSpec(memory_space=pltpu.HBM)] * 2 + [pl.BlockSpec(memory_space=pltpu.VMEM)] * 2,
        out_specs=(pl.BlockSpec(memory_space=pltpu.VMEM),) * 2,
        scratch_shapes=[pltpu.SemaphoreType.DMA((2, features // FOLD))],
        compiler_params=pltpu.CompilerParams(vmem_limit_bytes=SCOPED),
        cost_estimate=pl.CostEstimate(flops=2 * features * width, bytes_accessed=4 * features * width, transcendentals=0),
    )(gate, up, gain, code)


def stage_kernel(units, pieces, *refs):
    rows = refs[:pieces]
    weight_ref, head_ref, code_ref, unit_ref, before_ref, out_ref, block_ref = refs[pieces:]
    features = block_ref.shape[1]
    first, squares = 0, []
    for ref in rows:
        count = ref.shape[0]
        for at in range(0, count, 64):
            total = jnp.zeros((64, 128), jnp.float32)
            for lane in range(0, features, 128):
                part = ref[at : at + 64, lane : lane + 128]
                block_ref[first + at : first + at + 64, lane : lane + 128] = part
                part = part.astype(jnp.float32)
                total = total + part * part
            squares.append(jnp.sum(total, axis=1, keepdims=True))
        first += count
    inv_rms = lax.rsqrt(jnp.concatenate(squares, axis=0) / features + epsilon)

    gate = jnp.dot(block_ref[...], weight_ref[0], preferred_element_type=jnp.float32) * inv_rms
    up = jnp.dot(block_ref[...], weight_ref[1], preferred_element_type=jnp.float32) * inv_rms
    activated = gate / (1.0 + jnp.exp(-gate)) * up
    score = jnp.sum(activated * head_ref[...], axis=1, keepdims=True)

    rows = 8 * len(units)
    code = jnp.concatenate([code_ref[pl.ds(pl.multiple_of(unit_ref[at] * 8, 8), 8), :] for at in units], axis=0)
    owner, pack = code // 1024, code % 1024
    section = unit_ref[128]
    lane = lax.broadcasted_iota(jnp.int32, (rows, 128), 1)
    line = jnp.concatenate([owner // 8 == lane, pack // 32 + 32 * section == lane], axis=0)
    line = jnp.where(line, 1.0, 0.0).astype(jnp.bfloat16)
    slot = jnp.concatenate(
        [jnp.where(owner % 8 == lane, score, 0.0), jnp.where(pack % 32 + 8 == lane, score, 0.0)], axis=0
    )
    terms = []
    for _ in range(3):
        terms.append(slot.astype(jnp.bfloat16))
        slot = slot - terms[-1].astype(jnp.float32)
    placed = lax.dot_general(
        line, jnp.concatenate(terms, axis=1), (((0,), (0,)), ((), ())), preferred_element_type=jnp.float32
    )
    out_ref[...] = before_ref[...] + placed[:, 0:128] + placed[:, 128:256] + placed[:, 256:384]


def stage(pieces, weight, head, code, unit, before):
    _, features, width = weight.shape
    vmem = pl.BlockSpec(memory_space=pltpu.VMEM)
    arrays = [pltpu.with_memory_space_constraint(piece, pltpu.VMEM) for piece, _ in pieces]
    units = tuple(at for _, held in pieces for at in held)
    rows = 8 * len(units)
    weight = pltpu.with_memory_space_constraint(weight, pltpu.VMEM)
    code = pltpu.with_memory_space_constraint(code, pltpu.VMEM)
    return pl.pallas_call(
        functools.partial(stage_kernel, units, len(arrays)),
        out_shape=jax.ShapeDtypeStruct((128, 128), jnp.float32),
        in_specs=[vmem] * (len(arrays) + 3) + [pl.BlockSpec(memory_space=pltpu.SMEM), vmem],
        out_specs=vmem,
        scratch_shapes=[pltpu.VMEM((rows, features), jnp.bfloat16)],
        compiler_params=pltpu.CompilerParams(vmem_limit_bytes=SCOPED),
        cost_estimate=pl.CostEstimate(flops=4 * rows * features * width, bytes_accessed=4 * features * width, transcendentals=rows * width),
    )(*arrays, weight, head, code, unit, before)


def held(half, third, lines):
    return tuple(third * 32 + half * 16 + line * 4 + at for line in lines for at in range(4))


def unit_table(core, section):
    place = {"x": lax.axis_index("xh") * 2 + lax.axis_index("xl"), "y": lax.axis_index("y"), "z": lax.axis_index("z")}
    at = jnp.arange(128, dtype=jnp.int32)
    back = (at % 4, at // 4 % 4, at // 32)
    half = jnp.where(at // 16 % 2 == 0, core, 1 - core)
    device = []
    for kind in range(2):
        source = {axis: (place[axis] - back[phase]) % 4 for phase, axis in enumerate(ORDER[kind])}
        device.append(flat_index(source["x"], source["y"], source["z"], kind))
    table = jnp.where(half == 0, device[0], device[1])
    return jnp.concatenate([table, jnp.broadcast_to(section, (128,)).astype(jnp.int32)])


def finish_kernel(arrived_ref, unit_ref, scores_ref, joined_ref):
    def log_sigmoid(value):
        return jnp.minimum(value, 0.0) - jnp.log1p(jnp.exp(-jnp.abs(value)))

    sums = jnp.concatenate(
        [jnp.sum(arrived_ref[at : at + 32, :], axis=0, keepdims=True) for at in range(0, 128, 32)], axis=0
    )
    flipped = lax.broadcasted_iota(jnp.int32, sums.shape, 0) % 2 == 1
    joined_ref[...] = jnp.where(flipped, log_sigmoid(sums), sums)[:, 0:8]
    scores = jnp.sum(sums, axis=0, keepdims=True)
    scores_ref[...] = jnp.where(unit_ref[128] % 2 == 1, log_sigmoid(scores), scores)[:, 8:40]


def finish(arrived, unit):
    vmem = pl.BlockSpec(memory_space=pltpu.VMEM)
    return pl.pallas_call(
        finish_kernel,
        out_shape=(jax.ShapeDtypeStruct((1, 32), jnp.float32), jax.ShapeDtypeStruct((4, 8), jnp.float32)),
        in_specs=[vmem, pl.BlockSpec(memory_space=pltpu.SMEM)],
        out_specs=(vmem, vmem),
        compiler_params=pltpu.CompilerParams(vmem_limit_bytes=SCOPED),
    )(arrived, unit)


def exchange(sent):
    return lax.all_to_all(sent[:, None, :], ALL, split_axis=0, concat_axis=0, tiled=True).reshape(128, 128)


def body(hidden, norm_gain, gate_weight, up_weight, head_vector, pack_slot, owner_slot):
    core = lax.axis_index("core")
    section = lax.axis_index("xh") * 2 + core
    head = head_vector.astype(jnp.float32)
    own_pack = lax.dynamic_index_in_dim(pack_slot, section, 0, keepdims=False)
    code = (owner_slot * 1024 + own_pack).reshape(8, 128)
    unit = unit_table(core, section)
    sent = jnp.zeros((128, 128), jnp.float32)

    line = jnp.concatenate([hidden] + [shift(hidden, 0, step) for step in (1, 2, 3)], axis=0)
    line, gate, up, code, unit, head, sent = lax.optimization_barrier(
        (line, gate_weight[0], up_weight[0], code, unit, head, sent)
    )
    plane = jnp.concatenate([line] + [shift(line, 1, step) for step in (1, 2, 3)], axis=0)
    weight, code = fold(gate, up, norm_gain, code)
    plane, weight, code = lax.optimization_barrier((plane, weight, code))
    rest = (weight, head, code, unit)
    every = (0, 1, 2, 3)
    other = sibling(plane)
    behind = shift(plane, 2, 1)
    ahead = shift(plane, 2, 3)
    sent = stage(((plane, held(0, 0, every)), (other, held(1, 0, every))), *rest, sent)
    behind, ahead, sent = lax.optimization_barrier((behind, ahead, sent))
    far_low = shift(behind[:64], 2, 1)
    far_high = shift(ahead[64:], 2, 3)
    sent = stage(((behind, held(0, 1, every)), (sibling(behind), held(1, 1, every))), *rest, sent)
    sent = stage(((ahead, held(0, 3, every)), (sibling(ahead), held(1, 3, every))), *rest, sent)
    far_low, far_high, sent = lax.optimization_barrier((far_low, far_high, sent))
    far = ((sibling(far_low), held(1, 2, (0, 1))), (sibling(far_high), held(1, 2, (2, 3))))
    sent = stage(((far_low, held(0, 2, (0, 1))), (far_high, held(0, 2, (2, 3)))), *rest, sent)
    sent = stage(far, *rest, sent)

    return finish(exchange(sent), unit)


def solution(mesh):
    parts = Mesh(mesh.devices.reshape(2, 2, 2, 4, 4), ALL)
    section, shard = ("xh", "core"), ("xl", "z", "y")
    in_specs = (
        P(section + shard, None),
        P(section, None),
        P(section, None, shard),
        P(section, None, shard),
        P(section, shard),
        P(),
        P(),
    )
    out_specs = (P(section, shard), P(None, section + shard))
    return jax.shard_map(body, mesh=parts, in_specs=in_specs, out_specs=out_specs, check_vma=False)
```

```python
import functools

import jax
import jax.numpy as jnp
from jax import lax
from jax.experimental import pallas as pl
from jax.experimental.pallas import tpu as pltpu
from jax.sharding import Mesh, PartitionSpec as P

epsilon = 1e-06
ALL = ("xh", "core", "xl", "z", "y")
ORDER = (("y", "x", "z"), ("z", "x", "y"))
FOLD = 1024
SCOPED = 12 * 1024 * 1024


def flat_index(x, y, z, core):
    return (x // 2) * 64 + core * 32 + (x % 2) * 16 + z * 4 + y


def shift_pairs(phase, step):
    pairs = []
    for core in range(2):
        at = "xyz".index(ORDER[core][phase])
        for x in range(4):
            for y in range(4):
                for z in range(4):
                    to = [x, y, z]
                    to[at] = (to[at] + step) % 4
                    pairs.append((flat_index(x, y, z, core), flat_index(*to, core)))
    return pairs


def shift(block, phase, step):
    return lax.ppermute(block, ALL, shift_pairs(phase, step))


def sibling(block):
    return lax.ppermute(block, "core", [(0, 1), (1, 0)])


def fold_kernel(gate_ref, up_ref, gain_ref, code_ref, out_ref, spread_ref, sems):
    features, width = gate_ref.shape
    for block in range(features // FOLD):
        at = pl.ds(block * FOLD, FOLD)
        for half, ref in enumerate((gate_ref, up_ref)):
            pltpu.make_async_copy(ref.at[at, :], out_ref.at[half, at, :], sems.at[half, block]).start()

    for row in range(code_ref.shape[0]):
        code = jnp.broadcast_to(code_ref[row : row + 1, :].astype(jnp.float32), (128, 128))
        spread_ref[row * 128 : row * 128 + 128, :] = jnp.transpose(code, (1, 0)).astype(jnp.int32)

    @pl.loop(0, features // FOLD)
    def _(block):
        for half, ref in enumerate((gate_ref, up_ref)):
            at = pl.ds(pl.multiple_of(block * FOLD, FOLD), FOLD)
            pltpu.make_async_copy(ref.at[at, :], out_ref.at[half, at, :], sems.at[half, block]).wait()
        for part in range(FOLD // 128):
            at = pl.multiple_of(block * FOLD + part * 128, 128)
            gain = jnp.transpose(jnp.broadcast_to(gain_ref[:, pl.ds(at, 128)], (128, 128)), (1, 0))
            gain = jnp.concatenate([gain] * (width // 128), axis=1)
            for half in range(2):
                value = out_ref[half, pl.ds(at, 128), :].astype(jnp.float32)
                out_ref[half, pl.ds(at, 128), :] = (value * gain).astype(jnp.bfloat16)


def fold(gate, up, gain, code):
    features, width = gate.shape
    gate, up = (pltpu.with_memory_space_constraint(half, pltpu.HBM) for half in (gate, up))
    return pl.pallas_call(
        fold_kernel,
        out_shape=(pltpu.VMEM((2, features, width), jnp.bfloat16), pltpu.VMEM((code.size, 128), jnp.int32)),
        in_specs=[pl.BlockSpec(memory_space=pltpu.HBM)] * 2 + [pl.BlockSpec(memory_space=pltpu.VMEM)] * 2,
        out_specs=(pl.BlockSpec(memory_space=pltpu.VMEM),) * 2,
        scratch_shapes=[pltpu.SemaphoreType.DMA((2, features // FOLD))],
        compiler_params=pltpu.CompilerParams(vmem_limit_bytes=SCOPED),
        cost_estimate=pl.CostEstimate(flops=2 * features * width, bytes_accessed=4 * features * width, transcendentals=0),
    )(gate, up, gain, code)


def stage_kernel(units, pieces, *refs):
    rows = refs[:pieces]
    weight_ref, head_ref, code_ref, unit_ref, before_ref, out_ref, block_ref = refs[pieces:]
    features = block_ref.shape[1]
    first, squares = 0, []
    for ref in rows:
        count = ref.shape[0]
        for at in range(0, count, 16):
            total = jnp.zeros((16, 128), jnp.float32)
            for lane in range(0, features, 128):
                part = ref[at : at + 16, lane : lane + 128]
                block_ref[first + at : first + at + 16, lane : lane + 128] = part
                part = part.astype(jnp.float32)
                total = total + part * part
            squares.append(jnp.sum(total, axis=1, keepdims=True))
        first += count
    inv_rms = lax.rsqrt(jnp.concatenate(squares, axis=0) / features + epsilon)

    gate = jnp.dot(block_ref[...], weight_ref[0], preferred_element_type=jnp.float32) * inv_rms
    up = jnp.dot(block_ref[...], weight_ref[1], preferred_element_type=jnp.float32) * inv_rms
    activated = gate / (1.0 + jnp.exp(-gate)) * up
    score = jnp.sum(activated * head_ref[...], axis=1, keepdims=True)

    rows = 8 * len(units)
    code = jnp.concatenate([code_ref[pl.ds(pl.multiple_of(unit_ref[at] * 8, 8), 8), :] for at in units], axis=0)
    owner, pack = code // 1024, code % 1024
    section = unit_ref[128]
    lane = lax.broadcasted_iota(jnp.int32, (rows, 128), 1)
    line = jnp.concatenate([owner // 8 == lane, pack // 32 + 32 * section == lane], axis=0)
    line = jnp.where(line, 1.0, 0.0).astype(jnp.bfloat16)
    slot = jnp.concatenate(
        [jnp.where(owner % 8 == lane, score, 0.0), jnp.where(pack % 32 + 8 == lane, score, 0.0)], axis=0
    )
    terms = []
    for _ in range(3):
        terms.append(slot.astype(jnp.bfloat16))
        slot = slot - terms[-1].astype(jnp.float32)
    placed = lax.dot_general(
        line, jnp.concatenate(terms, axis=1), (((0,), (0,)), ((), ())), preferred_element_type=jnp.float32
    )
    out_ref[...] = before_ref[...] + placed[:, 0:128] + placed[:, 128:256] + placed[:, 256:384]


def stage(pieces, weight, head, code, unit, before):
    _, features, width = weight.shape
    vmem = pl.BlockSpec(memory_space=pltpu.VMEM)
    arrays = [pltpu.with_memory_space_constraint(piece, pltpu.VMEM) for piece, _ in pieces]
    units = tuple(at for _, held in pieces for at in held)
    rows = 8 * len(units)
    weight = pltpu.with_memory_space_constraint(weight, pltpu.VMEM)
    code = pltpu.with_memory_space_constraint(code, pltpu.VMEM)
    return pl.pallas_call(
        functools.partial(stage_kernel, units, len(arrays)),
        out_shape=jax.ShapeDtypeStruct((128, 128), jnp.float32),
        in_specs=[vmem] * (len(arrays) + 3) + [pl.BlockSpec(memory_space=pltpu.SMEM), vmem],
        out_specs=vmem,
        scratch_shapes=[pltpu.VMEM((rows, features), jnp.bfloat16)],
        compiler_params=pltpu.CompilerParams(vmem_limit_bytes=SCOPED),
        cost_estimate=pl.CostEstimate(flops=4 * rows * features * width, bytes_accessed=4 * features * width, transcendentals=rows * width),
    )(*arrays, weight, head, code, unit, before)


def held(half, third, lines):
    return tuple(third * 32 + half * 16 + line * 4 + at for line in lines for at in range(4))


def both(pieces, units, rest, sent):
    others = [sibling(piece) for piece in pieces]
    sent = stage(list(zip(pieces, units(0))), *rest, sent)
    return stage(list(zip(others, units(1))), *rest, sent)


def unit_table(core, section):
    place = {"x": lax.axis_index("xh") * 2 + lax.axis_index("xl"), "y": lax.axis_index("y"), "z": lax.axis_index("z")}
    at = jnp.arange(128, dtype=jnp.int32)
    back = (at % 4, at // 4 % 4, at // 32)
    half = jnp.where(at // 16 % 2 == 0, core, 1 - core)
    device = []
    for kind in range(2):
        source = {axis: (place[axis] - back[phase]) % 4 for phase, axis in enumerate(ORDER[kind])}
        device.append(flat_index(source["x"], source["y"], source["z"], kind))
    table = jnp.where(half == 0, device[0], device[1])
    return jnp.concatenate([table, jnp.broadcast_to(section, (128,)).astype(jnp.int32)])


def finish_kernel(arrived_ref, unit_ref, scores_ref, joined_ref):
    def log_sigmoid(value):
        return jnp.minimum(value, 0.0) - jnp.log1p(jnp.exp(-jnp.abs(value)))

    sums = jnp.concatenate(
        [jnp.sum(arrived_ref[at : at + 32, :], axis=0, keepdims=True) for at in range(0, 128, 32)], axis=0
    )
    flipped = lax.broadcasted_iota(jnp.int32, sums.shape, 0) % 2 == 1
    joined_ref[...] = jnp.where(flipped, log_sigmoid(sums), sums)[:, 0:8]
    scores = jnp.sum(sums, axis=0, keepdims=True)
    scores_ref[...] = jnp.where(unit_ref[128] % 2 == 1, log_sigmoid(scores), scores)[:, 8:40]


def finish(arrived, unit):
    vmem = pl.BlockSpec(memory_space=pltpu.VMEM)
    return pl.pallas_call(
        finish_kernel,
        out_shape=(jax.ShapeDtypeStruct((1, 32), jnp.float32), jax.ShapeDtypeStruct((4, 8), jnp.float32)),
        in_specs=[vmem, pl.BlockSpec(memory_space=pltpu.SMEM)],
        out_specs=(vmem, vmem),
        compiler_params=pltpu.CompilerParams(vmem_limit_bytes=SCOPED),
    )(arrived, unit)


def exchange(sent):
    return lax.all_to_all(sent[:, None, :], ALL, split_axis=0, concat_axis=0, tiled=True).reshape(128, 128)


def body(hidden, norm_gain, gate_weight, up_weight, head_vector, pack_slot, owner_slot):
    core = lax.axis_index("core")
    section = lax.axis_index("xh") * 2 + core
    head = head_vector.astype(jnp.float32)
    own_pack = lax.dynamic_index_in_dim(pack_slot, section, 0, keepdims=False)
    code = (owner_slot * 1024 + own_pack).reshape(8, 128)
    unit = unit_table(core, section)
    sent = jnp.zeros((128, 128), jnp.float32)

    line = jnp.concatenate([hidden] + [shift(hidden, 0, step) for step in (1, 2, 3)], axis=0)
    line, gate, up, code, unit, head, sent = lax.optimization_barrier(
        (line, gate_weight[0], up_weight[0], code, unit, head, sent)
    )
    left, right = shift(line, 1, 1), shift(line, 1, 3)
    down, above = shift(line, 2, 1), shift(line, 2, 3)
    weight, code = fold(gate, up, norm_gain, code)
    to_up = jnp.concatenate([left, right, down[:16]], axis=0)
    to_down = jnp.concatenate([left, right, above[16:]], axis=0)
    remainder = jnp.concatenate([down[16:], above], axis=0)
    other_line = sibling(line)
    line, other_line, remainder, to_up, to_down, weight, code = lax.optimization_barrier(
        (line, other_line, remainder, to_up, to_down, weight, code)
    )
    rest = (weight, head, code, unit)

    across = shift(line, 1, 2)
    from_down, from_up = shift(to_up, 2, 1), shift(to_down, 2, 3)
    near = held(0, 0, (0,)), held(0, 0, (1, 3)) + held(0, 1, (0,))[:2], held(0, 1, (0,))[2:] + held(0, 3, (0,))
    other_near = held(1, 0, (0,)), held(1, 0, (1, 3)) + held(1, 1, (0,))[:2], held(1, 1, (0,))[2:] + held(1, 3, (0,))
    others = (other_line, sibling(to_up), sibling(remainder))
    sent = stage(list(zip((line, to_up, remainder), near)), *rest, sent)
    sent = stage(list(zip(others, other_near)), *rest, sent)
    across, from_down, from_up, sent = lax.optimization_barrier((across, from_down, from_up, sent))

    far = shift(jnp.concatenate([from_down[64:], from_up[64:]], axis=0), 1, 2)
    low = shift(jnp.concatenate([across, from_down[:32]], axis=0), 2, 1)
    high = shift(jnp.concatenate([across, from_up[32:64]], axis=0), 2, 3)
    own = (from_down, from_up, across)
    sent = both(
        own,
        lambda half: [
            held(half, 1, (1, 3)) + held(half, 2, (0,))[:2],
            held(half, 3, (1, 3)) + held(half, 2, (0,))[2:],
            held(half, 0, (2,)),
        ],
        rest,
        sent,
    )
    low, high, far, sent = lax.optimization_barrier((low, high, far, sent))
    sent = both(
        (low, high, far),
        lambda half: [
            held(half, 1, (2,)) + held(half, 2, (1,)),
            held(half, 3, (2,)) + held(half, 2, (3,)),
            held(half, 2, (2,)),
        ],
        rest,
        sent,
    )

    return finish(exchange(sent), unit)


def solution(mesh):
    parts = Mesh(mesh.devices.reshape(2, 2, 2, 4, 4), ALL)
    section, shard = ("xh", "core"), ("xl", "z", "y")
    in_specs = (
        P(section + shard, None),
        P(section, None),
        P(section, None, shard),
        P(section, None, shard),
        P(section, shard),
        P(),
        P(),
    )
    out_specs = (P(section, shard), P(None, section + shard))
    return jax.shard_map(body, mesh=parts, in_specs=in_specs, out_specs=out_specs, check_vma=False)
```
